32 devices in a mesh: segment: 4 (over z), seq: 4 (over x, core), mp: 2 (over y).
Axes of the slice: x: 2, y: 2, z: 4, core: 2. Of those that a mesh axis runs over, the one named last changes fastest.
Arguments:
- latents: bfloat16 [4, 4, 256, 4096], P('segment', 'seq', None, 'mp'), may hold values from -6 to 6
- w_qkv: bfloat16 [4, 4096, 3, 4096], P('segment', 'seq', None, 'mp'), may hold values from -1 to 1
- w_out: bfloat16 [4, 4096, 4096], P('segment', 'mp', 'seq'), may hold values from -0.09375 to 0.09375
- mod_shift: float32 [4, 4096], P('segment'), may hold values from -3 to 3
- mod_scale: float32 [4, 4096], P('segment'), may hold values from 0.1 to 1.9
- mod_gate: float32 [4, 4096], P('segment'), may hold values from 0.5 to 1.5
- counts: int32 [4, 4], P('segment'), may hold values from 64 to 256, as said below
Outputs:
- next_latents: bfloat16 [4, 4, 256, 4096], P('segment', 'seq', None, 'mp')
The draws below stay inside these ranges and needn't reach their ends.
Inputs may be any that keep to these rules, and one draw needn't show every extreme that they name: `counts`: in every section's clip at least one frame has all 256 patch positions valid.
All inputs are finite; a program needn't handle non-finite values.
Results may differ from the reference program's by a relative error of at most 0.01.
Values may be sent and summed in bfloat16 or wider, within the bound.
A program may use at most 192 MiB of HBM per device.

```python
import math
import jax
import jax.numpy as jnp
from jax import lax

D = 4096
HEADS = 32
HD = 128
P_SIZE = 256
FRAMES = 4
SEGMENTS = 4
N_MP = 2


def draw_latents(key, part):
    shape = (SEGMENTS, FRAMES, P_SIZE, D)
    return jnp.clip(jax.random.normal(jax.random.fold_in(key, 23), shape, dtype=jnp.float32), -6.0, 6.0).astype(jnp.bfloat16)


def draw_w_qkv(key, part):
    shape = (SEGMENTS, D, 3, HEADS * HD)
    return (jnp.clip(jax.random.normal(jax.random.fold_in(key, 33), shape, dtype=jnp.float32), -5.0, 5.0) / math.sqrt(D)).astype(jnp.bfloat16)


def draw_counts(key, part):
    base = jax.random.randint(jax.random.fold_in(key, 3), (SEGMENTS, FRAMES), P_SIZE // 4, P_SIZE + 1)
    full_frame = jax.random.randint(jax.random.fold_in(key, 5), (SEGMENTS, 1), 0, FRAMES)
    return jnp.where(jnp.arange(FRAMES)[None, :] == full_frame, P_SIZE, base).astype(jnp.int32)


def level_of(stream_key, dims, pieces, least, largest):
    def one(axis_at, shards_of):
        draws = jax.random.uniform(jax.random.fold_in(jax.random.fold_in(stream_key, 6), axis_at), (shards_of,), jnp.float32, least / len(pieces), largest / len(pieces))
        return jnp.repeat(jnp.exp(draws), dims[axis_at] // shards_of).reshape((-1,) + (1,) * (len(dims) - axis_at - 1))

    level = one(*pieces[0])
    for cut in pieces[1:]:
        level = level * one(*cut)
    return level


def scatter_about(rng, extent, scale, most, cuts=(), kind=jnp.bfloat16):
    loudness = level_of(rng, extent, cuts, -0.22, 0.18) if cuts else 1.0
    drawn = jax.random.normal(rng, extent, jnp.float32) * scale * loudness
    return jnp.minimum(jnp.maximum(drawn, -most), most).astype(kind)


def setup_inputs(seed: int = 0) -> dict:
    keys = jax.random.split(jax.random.key(seed), 8)
    return {
        "latents": draw_latents(jax.random.fold_in(keys[7], 71), 0),
        "w_qkv": draw_w_qkv(jax.random.fold_in(keys[7], 71), 0),
        "w_out": scatter_about(keys[2], (SEGMENTS, HEADS * HD, D), (HEADS * HD) ** -0.5, 0.09375, ((0, 4), (1, 2), (2, 4))),
        "mod_shift": scatter_about(keys[3], (SEGMENTS, D), 0.5, 3.0, ((0, 4),), jnp.float32),
        "mod_scale": jnp.clip(1.0 + 0.18 * jax.random.normal(keys[4], (SEGMENTS, D), jnp.float32), 0.1, 1.9),
        "mod_gate": jnp.clip(0.5 + 1.0 * jax.random.uniform(keys[5], (SEGMENTS, D), jnp.float32) ** level_of(keys[5], (SEGMENTS, D), ((0, 4),), -0.2, 0.2), 0.5, 1.5),
        "counts": draw_counts(jax.random.fold_in(keys[7], 71), 0),
    }


EPS = 1e-06
NEG_FILL = -1e+30

def masked_attention(queries, keys_in, values, usable):
    factor = 1.0 / math.sqrt(queries.shape[-1])
    scores = jnp.einsum('...ihe,...jhe->...hij', queries.astype(jnp.float32), keys_in.astype(jnp.float32)) * factor
    allowed = usable[..., None, :, None] & usable[..., None, None, :]
    masked = jnp.where(allowed, scores, NEG_FILL)
    highest = lax.optimization_barrier(jnp.max(masked, axis=-1, keepdims=True))
    raised = jnp.where(allowed, jnp.exp(masked - highest), 0.0)
    spare_one = jnp.where(usable, 0.0, 1.0)[..., None, :, None]
    weights = (raised / (lax.optimization_barrier(jnp.sum(raised, axis=-1, keepdims=True)) + spare_one)).astype(jnp.bfloat16)
    blended = jnp.einsum('...hij,...jhe->...ihe', weights.astype(jnp.float32), values.astype(jnp.float32))
    return blended.astype(jnp.bfloat16)

def section(block_rows, w_in, w_proj, shift_vec, scale_vec, gate_vec, clip_counts, spatial):
    frames = block_rows.shape[0]
    patches = block_rows.shape[1]
    span = patches // frames
    widened = block_rows.astype(jnp.float32)
    average = lax.optimization_barrier(jnp.mean(widened, axis=-1, keepdims=True))
    centred = widened - average
    variance = lax.optimization_barrier(jnp.mean(centred * centred, axis=-1, keepdims=True))
    modulated = (centred * lax.rsqrt(variance + EPS) * scale_vec + shift_vec).astype(jnp.bfloat16)
    projected = jnp.dot(modulated.reshape(-1, D), w_in.reshape(D, -1), preferred_element_type=jnp.float32)
    projected = projected.astype(jnp.bfloat16).reshape(frames, patches, 3, HEADS, HD)
    if spatial:
        usable = jnp.arange(patches)[None, :] < clip_counts[:, None]
        attended = lax.map(lambda member: masked_attention(member[0], member[1], member[2], member[3]), (projected[:, :, 0], projected[:, :, 1], projected[:, :, 2], usable))
    else:
        by_place = projected.reshape(frames, frames, span, 3, HEADS, HD).transpose(0, 2, 1, 3, 4, 5)
        location = jnp.arange(frames)[:, None] * span + jnp.arange(span)[None, :]
        usable = location[:, :, None] < clip_counts[None, None, :]
        attended = masked_attention(by_place[:, :, :, 0], by_place[:, :, :, 1], by_place[:, :, :, 2], usable)
        attended = attended.transpose(0, 2, 1, 3, 4)
    attended = attended.reshape(frames * patches, HEADS * HD)
    per_group = HEADS * HD // N_MP
    branch = jnp.zeros((frames * patches, D), jnp.float32)
    for member in range(N_MP):
        partial_value = jnp.dot(attended[:, member * per_group:(member + 1) * per_group], w_proj[member * per_group:(member + 1) * per_group], preferred_element_type=jnp.float32)
        rounded = lax.optimization_barrier(partial_value.astype(jnp.bfloat16))
        branch = branch + rounded.astype(jnp.float32)
    updated = (widened.reshape(-1, D) + gate_vec * branch).astype(jnp.bfloat16)
    return updated.reshape(frames, frames, span, D).transpose(1, 0, 2, 3).reshape(frames, patches, D)

def reference(latents, w_qkv, w_out, mod_shift, mod_scale, mod_gate, counts):
    results = []
    for section_id in range(SEGMENTS):
        results.append(section(latents[section_id], w_qkv[section_id], w_out[section_id], mod_shift[section_id], mod_scale[section_id], mod_gate[section_id], counts[section_id], section_id % 2 == 0))
    moved = [results[(member - 1) % SEGMENTS] for member in range(SEGMENTS)]
    return jnp.stack(moved)
```

```python
import math

import jax
import jax.numpy as jnp
from jax import lax
from jax.sharding import PartitionSpec as P

HD = 128


EPS = 1e-06
NEG_FILL = -1e30


def passed_along(x, axis, by):
    length = lax.axis_size(axis)
    return lax.ppermute(x, axis, [(i, (i + by) % length) for i in range(length)])


def masked_attention(queries, keys_in, values, usable):
    factor = 1.0 / math.sqrt(queries.shape[-1])
    scores = (
        jnp.einsum("...ihe,...jhe->...hij", queries, keys_in, preferred_element_type=jnp.float32)
        * factor
    )
    allowed = usable[..., None, :, None] & usable[..., None, None, :]
    masked = jnp.where(allowed, scores, NEG_FILL)
    highest = jnp.max(masked, axis=-1, keepdims=True)
    raised = jnp.where(allowed, jnp.exp(masked - highest), 0.0)
    spare_one = jnp.where(usable, 0.0, 1.0)[..., None, :, None]
    weights = (raised / (jnp.sum(raised, axis=-1, keepdims=True) + spare_one)).astype(jnp.bfloat16)
    blended = jnp.einsum(
        "...hij,...jhe->...ihe", weights, values, preferred_element_type=jnp.float32
    )
    return blended.astype(jnp.bfloat16)


def relay_features(rows_now):
    return lax.all_to_all(rows_now, "seq", split_axis=0, concat_axis=0, tiled=True)


def pass_onward(rows_now):
    return passed_along(rows_now, "segment", 1)


def on_device(latents, w_qkv, w_out, mod_shift, mod_scale, mod_gate, counts):
    frames = lax.axis_size("seq")
    patches = latents.shape[2]
    narrow = latents.shape[3]
    span = patches // frames
    segment_rows = latents[0, 0]
    gathered = lax.all_gather(latents, "mp", axis=3, tiled=True)[0, 0]
    residual = relay_features(segment_rows.reshape(frames, span, narrow))
    widened = gathered.astype(jnp.float32)
    average = jnp.mean(widened, axis=-1, keepdims=True)
    centred = widened - average
    variance = jnp.mean(centred * centred, axis=-1, keepdims=True)
    modulated = (centred * lax.rsqrt(variance + EPS) * mod_scale[0] + mod_shift[0]).astype(
        jnp.bfloat16
    )
    columns = w_qkv.shape[2] * w_qkv.shape[3]
    depth = w_qkv.shape[1]
    spread = lax.all_to_all(
        modulated.reshape(patches, frames, depth).transpose(1, 0, 2),
        "seq", split_axis=0, concat_axis=0, tiled=True,
    ).reshape(frames * patches, depth)
    partial_in = jnp.dot(
        spread, w_qkv[0].reshape(depth, columns), preferred_element_type=jnp.float32
    ).astype(jnp.bfloat16)
    projected = lax.psum_scatter(partial_in, "seq", scatter_dimension=0, tiled=True)
    local_heads = w_qkv.shape[3] // HD
    projected = projected.reshape(patches, 3, local_heads, HD)
    frame_here = lax.axis_index("seq")
    clip_counts = counts[0]
    positions = jnp.arange(frames)

    def spatial(triple):
        count_here = jnp.sum(jnp.where(positions == frame_here, clip_counts, 0))
        usable = jnp.arange(patches) < count_here
        return masked_attention(triple[:, 0], triple[:, 1], triple[:, 2], usable)

    def temporal(triple):
        by_place = triple.reshape(frames, span, 3, local_heads, HD).transpose(1, 0, 2, 3, 4)
        location = frame_here * span + jnp.arange(span)
        usable = location[:, None] < clip_counts[None, :]
        blended = masked_attention(by_place[:, :, 0], by_place[:, :, 1], by_place[:, :, 2], usable)
        return blended.transpose(1, 0, 2, 3).reshape(patches, local_heads, HD)

    attended = lax.cond(lax.axis_index("segment") % 2 == 0, spatial, temporal, projected)
    attended = attended.reshape(patches, local_heads * HD)
    attended = lax.all_gather(attended, "seq", axis=0, tiled=True)
    member = lax.axis_index("mp")
    partials = jnp.dot(attended, w_out[0], preferred_element_type=jnp.float32).astype(jnp.bfloat16)
    width = w_out.shape[2]
    outgoing = partials.reshape(frames, frames, span, width).transpose(1, 0, 2, 3)
    arrived = lax.all_to_all(
        outgoing.reshape(frames, patches, width), "seq", split_axis=0, concat_axis=0, tiled=True
    )
    summed = lax.psum_scatter(arrived, "mp", scatter_dimension=0, tiled=True)
    summed = summed.transpose(1, 0, 2).reshape(patches, narrow).astype(jnp.float32)
    gate_here = lax.dynamic_slice_in_dim(mod_gate[0], member * narrow, narrow)
    updated = residual.reshape(patches, narrow).astype(jnp.float32) + gate_here * summed
    moved = pass_onward(updated.astype(jnp.bfloat16))
    return moved.reshape(1, 1, patches, narrow)


def solution(mesh):
    return jax.shard_map(
        on_device,
        mesh=mesh,
        in_specs=(
            P("segment", "seq", None, "mp"),
            P("segment", "seq", None, "mp"),
            P("segment", "mp", "seq"),
            P("segment", None),
            P("segment", None),
            P("segment", None),
            P("segment", None),
        ),
        out_specs=P("segment", "seq", None, "mp"),
        check_vma=False,
    )
```

```python
import functools
import math

import jax
import jax.numpy as jnp
from jax import lax
from jax.experimental import pallas as pl
from jax.experimental.pallas import tpu as pltpu
from jax.sharding import PartitionSpec as P

HD = 128


EPS = 1e-06
NEG_FILL = -1e30


def passed_along(x, axis, by):
    length = lax.axis_size(axis)
    return lax.ppermute(x, axis, [(i, (i + by) % length) for i in range(length)])


def masked_attention(queries, keys_in, values, usable):
    factor = 1.0 / math.sqrt(queries.shape[-1])
    scores = (
        jnp.einsum("...ihe,...jhe->...hij", queries, keys_in, preferred_element_type=jnp.float32)
        * factor
    )
    allowed = usable[..., None, :, None] & usable[..., None, None, :]
    masked = jnp.where(allowed, scores, NEG_FILL)
    highest = jnp.max(masked, axis=-1, keepdims=True)
    raised = jnp.where(allowed, jnp.exp(masked - highest), 0.0)
    spare_one = jnp.where(usable, 0.0, 1.0)[..., None, :, None]
    weights = (raised / (jnp.sum(raised, axis=-1, keepdims=True) + spare_one)).astype(jnp.bfloat16)
    blended = jnp.einsum(
        "...hij,...jhe->...ihe", weights, values, preferred_element_type=jnp.float32
    )
    return blended.astype(jnp.bfloat16)


def relay_features(rows_now):
    return lax.all_to_all(rows_now, "seq", split_axis=0, concat_axis=0, tiled=True)


def pass_onward(rows_now):
    return passed_along(rows_now, "segment", 1)


def on_device(latents, w_qkv, w_out, mod_shift, mod_scale, mod_gate, counts):
    frames = lax.axis_size("seq")
    patches = latents.shape[2]
    narrow = latents.shape[3]
    span = patches // frames
    segment_rows = latents[0, 0]
    gathered = lax.all_gather(latents, "mp", axis=3, tiled=True)[0, 0]
    residual = relay_features(segment_rows.reshape(frames, span, narrow))
    widened = gathered.astype(jnp.float32)
    average = jnp.mean(widened, axis=-1, keepdims=True)
    centred = widened - average
    variance = jnp.mean(centred * centred, axis=-1, keepdims=True)
    modulated = (centred * lax.rsqrt(variance + EPS) * mod_scale[0] + mod_shift[0]).astype(
        jnp.bfloat16
    )
    columns = w_qkv.shape[2] * w_qkv.shape[3]
    depth = w_qkv.shape[1]
    spread = lax.all_to_all(
        modulated.reshape(patches, frames, depth).transpose(1, 0, 2),
        "seq", split_axis=0, concat_axis=0, tiled=True,
    ).reshape(frames * patches, depth)
    partial_in = jnp.dot(
        spread, w_qkv[0].reshape(depth, columns), preferred_element_type=jnp.float32
    ).astype(jnp.bfloat16)
    projected = lax.psum_scatter(partial_in, "seq", scatter_dimension=0, tiled=True)
    local_heads = w_qkv.shape[3] // HD
    projected = projected.reshape(patches, 3, local_heads, HD)
    frame_here = lax.axis_index("seq")
    clip_counts = counts[0]
    positions = jnp.arange(frames)

    def spatial(triple):
        count_here = jnp.sum(jnp.where(positions == frame_here, clip_counts, 0))
        usable = jnp.arange(patches) < count_here
        return masked_attention(triple[:, 0], triple[:, 1], triple[:, 2], usable)

    def temporal(triple):
        by_place = triple.reshape(frames, span, 3, local_heads, HD).transpose(1, 0, 2, 3, 4)
        location = frame_here * span + jnp.arange(span)
        usable = location[:, None] < clip_counts[None, :]
        blended = masked_attention(by_place[:, :, 0], by_place[:, :, 1], by_place[:, :, 2], usable)
        return blended.transpose(1, 0, 2, 3).reshape(patches, local_heads, HD)

    attended = lax.cond(lax.axis_index("segment") % 2 == 0, spatial, temporal, projected)
    attended = attended.reshape(patches, local_heads * HD)
    attended = lax.all_gather(attended, "seq", axis=0, tiled=True)
    member = lax.axis_index("mp")
    partials = jnp.dot(attended, w_out[0], preferred_element_type=jnp.float32).astype(jnp.bfloat16)
    width = w_out.shape[2]
    outgoing = partials.reshape(frames, frames, span, width).transpose(1, 0, 2, 3)
    arrived = lax.all_to_all(
        outgoing.reshape(frames, patches, width), "seq", split_axis=0, concat_axis=0, tiled=True
    )
    summed = lax.psum_scatter(arrived, "mp", scatter_dimension=0, tiled=True)
    summed = summed.transpose(1, 0, 2).reshape(patches, narrow).astype(jnp.float32)
    gate_here = lax.dynamic_slice_in_dim(mod_gate[0], member * narrow, narrow)
    updated = residual.reshape(patches, narrow).astype(jnp.float32) + gate_here * summed
    moved = pass_onward(updated.astype(jnp.bfloat16))
    return moved.reshape(1, 1, patches, narrow)


CHUNKS = 4


def whole_kernel(
    x, wq, wo, shift, scale, gate, counts, out,
    w_in, w_proj, tokens, mod, stats, heads, sent, came, own, outs, parts, rest,
    stat_send, stat_recv, wl, ws, wr, wol, m_send, m_recv, f_send, f_recv,
    p_send, p_recv, ax_send, ax_recv, as_send, as_recv, af_send, af_recv,
    o_send, o_recv, r_send, r_recv,
):
    seg, j, m = lax.axis_index("segment"), lax.axis_index("seq"), lax.axis_index("mp")
    n_seg, n_seq, n_mp = lax.axis_size("segment"), lax.axis_size("seq"), lax.axis_size("mp")
    side, core = j // 2, j % 2
    sib = side * 2 + 1 - core
    across = (1 - side) * 2 + core
    after, before = lax.rem(seg + 1, n_seg), lax.rem(seg + n_seg - 1, n_seg)
    patches, narrow = x.shape
    span = patches // n_seq
    depth = wq.shape[1]
    wide = wq.shape[2] // 2
    step = wide // CHUNKS
    rows = 2 * patches

    def remote(src, dst, send, recv, seq=None, mp=None, segment=None):
        return pltpu.make_async_remote_copy(
            src_ref=src, dst_ref=dst, send_sem=send, recv_sem=recv,
            device_id=(seg if segment is None else segment, j if seq is None else seq,
                       m if mp is None else mp),
            device_id_type=pl.DeviceIdType.MESH,
        )

    def arrived(dst, recv, send):
        remote(dst, dst, send, recv, seq=sib).wait_recv()

    barrier = pltpu.get_barrier_semaphore()
    for dj in range(n_seq):
        for dm in range(n_mp):
            if dj or dm:
                pl.semaphore_signal(
                    barrier, inc=1,
                    device_id=(seg, lax.rem(j + dj, n_seq), lax.rem(m + dm, n_mp)),
                    device_id_type=pl.DeviceIdType.MESH,
                )
            pl.semaphore_signal(
                barrier, inc=1, device_id=(before, dj, dm), device_id_type=pl.DeviceIdType.MESH
            )

    def columns(which, g):
        return pl.ds(pl.multiple_of(which * wide + g * step, step), step)

    def w_local(g):
        return pltpu.make_async_copy(wq.at[:, :, columns(core, g)], w_in.at[g, :, core], wl.at[g])

    def w_remote(g):
        return remote(
            wq.at[:, :, columns(1 - core, g)], w_in.at[g, :, core], ws.at[g], wr.at[g], seq=sib
        )

    for g in range(CHUNKS):
        w_local(g).start()
    proj_copy = pltpu.make_async_copy(wo, w_proj, wol)
    proj_copy.start()

    values = x[...].astype(jnp.float32)
    mean_here = jnp.mean(values, axis=-1, keepdims=True)
    off = values - mean_here
    square_here = jnp.sum(off * off, axis=-1, keepdims=True)
    lane = lax.broadcasted_iota(jnp.int32, (patches, 128), 1)
    stats[0] = jnp.where(lane < 64, mean_here, square_here)

    pl.semaphore_wait(barrier, n_seq * n_mp * 2 - 1)

    stat_copy = remote(stats.at[0], stats.at[1], stat_send, stat_recv, mp=1 - m)
    stat_copy.start()
    for g in range(CHUNKS):
        w_remote(g).start()

    def rest_copy(b):
        return remote(
            x.at[pl.ds(b * span, span)],
            rest.at[pl.ds(pl.multiple_of(j * span, span), span)],
            r_send.at[b], r_recv.at[j], seq=b, segment=after,
        )

    stat_copy.wait()
    mean_there = stats[1, :, 0:1]
    square_there = stats[1, :, 127:128]
    mean = (mean_here + mean_there) * 0.5
    gap = mean_here - mean_there
    variance = (square_here + square_there + gap * gap * (0.5 * narrow)) / (2.0 * narrow)
    rstd = lax.rsqrt(variance + EPS)

    def m_copy(q, y):
        return remote(
            mod.at[q], tokens.at[q, j], m_send.at[q, y], m_recv.at[j], seq=m * 2 + q, mp=y
        )

    for q in range(2):
        at = pl.ds(pl.multiple_of(m * narrow + q * depth, depth), depth)
        block = x[:, q * depth:(q + 1) * depth].astype(jnp.float32)
        mod[q] = ((block - mean) * rstd * scale[:, at] + shift[:, at]).astype(jnp.bfloat16)
        for y in range(2):
            mine = jnp.logical_and(jnp.logical_and(side == m, core == q), m == y)

            @pl.when(jnp.logical_not(mine))
            def _():
                m_copy(q, y).start()

            @pl.when(mine)
            def _():
                tokens[q, j] = mod[q]

    for b in range(n_seq):
        rest_copy(b).start()

    def f_copy(t):
        return remote(tokens.at[core, t], tokens.at[core, t], f_send.at[t], f_recv.at[t], seq=sib)

    def pass_token(t):
        @pl.when(jnp.logical_not(jnp.logical_and(side == m, t == j)))
        def _():
            arrived(tokens.at[core, t], m_recv.at[t], f_send.at[t])

        f_copy(t).start()

    def got_token(t):
        arrived(tokens.at[1 - core, t], f_recv.at[t], f_send.at[t])

    def project(which, g, i):
        total = jnp.zeros((rows, step), jnp.float32)
        for k in range(2):
            total = total + jnp.dot(
                tokens[k, pl.ds(which * 2, 2)].reshape(rows, depth), w_in[g, i, k],
                preferred_element_type=jnp.float32,
            )
        return total

    for t in range(2):
        pass_token(side * 2 + t)
    for t in range(2):
        got_token(side * 2 + t)

    def own_step(g, carry):
        w_local(g).wait()
        w_remote(g).wait_send()
        arrived(w_in.at[g, :, 1 - core], wr.at[g], ws.at[g])
        for i in range(3):
            own[g, i] = project(side, g, i)
        return carry

    lax.fori_loop(0, CHUNKS, own_step, 0)

    for t in range(2):
        pass_token((1 - side) * 2 + t)
    for t in range(2):
        got_token((1 - side) * 2 + t)

    def p_copy(g):
        return remote(sent.at[g], came.at[g], p_send.at[g], p_recv.at[g], seq=across)

    def send_step(g, carry):
        for i in range(3):
            sent[g, i] = project(1 - side, g, i).astype(jnp.bfloat16)
        p_copy(g).start()
        return carry

    lax.fori_loop(0, CHUNKS, send_step, 0)

    spatial = 1 - lax.rem(seg, 2)

    def places(r, t):
        frame = jnp.zeros_like(r)
        for f in range(1, n_seq):
            frame = frame + jnp.where(r >= f * span, 1, 0)
        spot = r - frame * span
        frame = spatial * t + (1 - spatial) * frame
        patch = spatial * r + (1 - spatial) * (t * span + spot)
        limit = jnp.zeros_like(r)
        for f in range(n_seq):
            limit = jnp.where(frame == f, counts[0, f], limit)
        return patch < limit, (1 - spatial) * spot

    def ax_copy(g):
        here = heads.at[core, g, pl.ds(side * 2, 2)]
        return remote(here, here, ax_send.at[g], ax_recv.at[g], seq=across)

    def as_copy(g):
        here = heads.at[core, g, pl.ds(side * 2, 2)]
        return remote(here, here, as_send.at[g], as_recv.at[g], seq=sib)

    def af_copy(g):
        here = heads.at[core, g, pl.ds((1 - side) * 2, 2)]
        return remote(here, here, af_send.at[g], af_recv.at[g], seq=sib)

    def forward(g):
        arrived(heads.at[core, g, pl.ds((1 - side) * 2, 2)], ax_recv.at[g], af_send.at[g])
        af_copy(g).start()

    factor = 1.0 / math.sqrt(HD)

    def attend_step(g, carry):
        p_copy(g).wait_send()
        arrived(came.at[g], p_recv.at[g], p_send.at[g])
        for b in range(2):
            t = side * 2 + b
            valid_q, spot_q = places(lax.broadcasted_iota(jnp.int32, (patches, 1), 0), t)
            valid_k, spot_k = places(lax.broadcasted_iota(jnp.int32, (1, patches), 1), t)
            allowed = jnp.logical_and(jnp.logical_and(valid_q, valid_k), spot_q == spot_k)
            spare = jnp.where(valid_q, 0.0, 1.0)
            mine = pl.ds(b * patches, patches)
            q, k, v = [
                (own[g, i, mine] + came[g, i, mine].astype(jnp.float32)).astype(jnp.bfloat16)
                for i in range(3)
            ]
            for h in range(step // HD):
                at = slice(h * HD, (h + 1) * HD)
                scores = lax.dot_general(
                    q[:, at], k[:, at], (((1,), (1,)), ((), ())),
                    preferred_element_type=jnp.float32,
                ) * factor
                masked = jnp.where(allowed, scores, NEG_FILL)
                highest = jnp.max(masked, axis=-1, keepdims=True)
                raised = jnp.where(allowed, jnp.exp(masked - highest), 0.0)
                total = jnp.sum(raised, axis=-1, keepdims=True) + spare
                weights = (raised / total).astype(jnp.bfloat16)
                blended = jnp.dot(weights, v[:, at], preferred_element_type=jnp.float32)
                heads[core, g, t, :, :, at] = blended.astype(jnp.bfloat16).reshape(n_seq, span, HD)
        ax_copy(g).start()
        as_copy(g).start()

        @pl.when(g > 0)
        def _():
            forward(g - 1)

        return carry

    lax.fori_loop(0, CHUNKS, attend_step, 0)
    forward(CHUNKS - 1)
    for g in range(CHUNKS):
        arrived(heads.at[1 - core, g, pl.ds(side * 2, 2)], as_recv.at[g], as_send.at[g])
        arrived(heads.at[1 - core, g, pl.ds((1 - side) * 2, 2)], af_recv.at[g], af_send.at[g])
    proj_copy.wait()

    gate_here = gate[:, pl.ds(pl.multiple_of(j * depth, depth), depth)]

    def o_copy(b):
        return remote(
            outs.at[b], parts.at[core, m], o_send.at[b], o_recv.at[core, m],
            seq=b, mp=side, segment=after,
        )

    def out_step(b, carry):
        left = jnp.concatenate(
            [heads[k, g, :, b].reshape(patches, step) for k in range(2) for g in range(CHUNKS)],
            axis=-1,
        )
        half = depth // 2
        for n in range(2):
            at = slice(n * half, (n + 1) * half)
            branch = jnp.dot(left, w_proj[:, at], preferred_element_type=jnp.float32)
            outs[b, :, at] = (branch * gate_here[:, at]).astype(jnp.bfloat16)
        o_copy(b).start()
        return carry

    lax.fori_loop(0, n_seq, out_step, 0)

    for f in range(n_seq):
        arrived(rest.at[pl.ds(f * span, span)], r_recv.at[f], r_send.at[f])
    for q in range(2):
        for y in range(2):
            arrived(parts.at[q, y], o_recv.at[q, y], o_send.at[q])
        at = slice(q * depth, (q + 1) * depth)
        out[:, at] = (
            rest[:, at].astype(jnp.float32)
            + parts[q, 0].astype(jnp.float32) + parts[q, 1].astype(jnp.float32)
        ).astype(jnp.bfloat16)

    for q in range(2):
        for y in range(2):
            @pl.when(jnp.logical_not(
                jnp.logical_and(jnp.logical_and(side == m, core == q), m == y)
            ))
            def _():
                m_copy(q, y).wait_send()
    for t in range(n_seq):
        f_copy(t).wait_send()
        rest_copy(t).wait_send()
        o_copy(t).wait_send()
    for g in range(CHUNKS):
        ax_copy(g).wait_send()
        as_copy(g).wait_send()
        af_copy(g).wait_send()


def in_one_kernel(latents, w_qkv, w_out, mod_shift, mod_scale, mod_gate, counts):
    patches, narrow = latents.shape[2:]
    n_seq = lax.axis_size("seq")
    depth, heads_wide = w_qkv.shape[1], w_qkv.shape[3]
    wide = heads_wide // 2
    step = wide // CHUNKS
    span = patches // n_seq
    rows = 2 * patches
    vmem = pl.BlockSpec(memory_space=pltpu.VMEM)
    dma = pltpu.SemaphoreType.DMA
    bf16 = jnp.bfloat16
    moved = pl.pallas_call(
        whole_kernel,
        out_shape=jax.ShapeDtypeStruct((patches, narrow), bf16),
        in_specs=[
            vmem, pl.BlockSpec(memory_space=pl.ANY), pl.BlockSpec(memory_space=pl.ANY),
            vmem, vmem, vmem, pl.BlockSpec(memory_space=pltpu.SMEM),
        ],
        out_specs=vmem,
        scratch_shapes=[
            pltpu.VMEM((CHUNKS, 3, 2, depth, step), bf16),
            pltpu.VMEM(w_out.shape[1:], bf16),
            pltpu.VMEM((2, n_seq, patches, depth), bf16),
            pltpu.VMEM((2, patches, depth), bf16),
            pltpu.VMEM((2, patches, 128), jnp.float32),
            pltpu.VMEM((2, CHUNKS, n_seq, n_seq, span, step), bf16),
            pltpu.VMEM((CHUNKS, 3, rows, step), bf16),
            pltpu.VMEM((CHUNKS, 3, rows, step), bf16),
            pltpu.VMEM((CHUNKS, 3, rows, step), jnp.float32),
            pltpu.VMEM((n_seq, patches, depth), bf16),
            pltpu.VMEM((2, 2, patches, depth), bf16),
            pltpu.VMEM((patches, narrow), bf16),
            dma, dma, dma((CHUNKS,)), dma((CHUNKS,)), dma((CHUNKS,)), dma,
            dma((2, 2)), dma((n_seq,)), dma((n_seq,)), dma((n_seq,)),
            dma((CHUNKS,)), dma((CHUNKS,)), dma((CHUNKS,)), dma((CHUNKS,)),
            dma((CHUNKS,)), dma((CHUNKS,)), dma((CHUNKS,)), dma((CHUNKS,)),
            dma((n_seq,)), dma((2, 2)), dma((n_seq,)), dma((n_seq,)),
        ],
        compiler_params=pltpu.CompilerParams(
            collective_id=0, has_side_effects=True, vmem_limit_bytes=60 * 2**20
        ),
    )(
        latents[0, 0], w_qkv[0].transpose(1, 0, 2), w_out[0],
        mod_shift, mod_scale, mod_gate, counts,
    )
    return moved.reshape(latents.shape)


def solution(mesh):
    square = mesh.shape["seq"] == 4 and mesh.shape["mp"] == 2
    return jax.shard_map(
        in_one_kernel if square else on_device,
        mesh=mesh,
        in_specs=(
            P("segment", "seq", None, "mp"),
            P("segment", "seq", None, "mp"),
            P("segment", "mp", "seq"),
            P("segment", None),
            P("segment", None),
            P("segment", None),
            P("segment", None),
        ),
        out_specs=P("segment", "seq", None, "mp"),
        check_vma=False,
    )
```

```python
import math

import jax
import jax.numpy as jnp
from jax import lax
from jax.experimental import pallas as pl
from jax.experimental.pallas import tpu as pltpu
from jax.sharding import PartitionSpec as P

HD = 128


EPS = 1e-06
NEG_FILL = -1e30


def passed_along(x, axis, by):
    length = lax.axis_size(axis)
    return lax.ppermute(x, axis, [(i, (i + by) % length) for i in range(length)])


def masked_attention(queries, keys_in, values, usable):
    factor = 1.0 / math.sqrt(queries.shape[-1])
    scores = (
        jnp.einsum("...ihe,...jhe->...hij", queries, keys_in, preferred_element_type=jnp.float32)
        * factor
    )
    allowed = usable[..., None, :, None] & usable[..., None, None, :]
    masked = jnp.where(allowed, scores, NEG_FILL)
    highest = jnp.max(masked, axis=-1, keepdims=True)
    raised = jnp.where(allowed, jnp.exp(masked - highest), 0.0)
    spare_one = jnp.where(usable, 0.0, 1.0)[..., None, :, None]
    weights = (raised / (jnp.sum(raised, axis=-1, keepdims=True) + spare_one)).astype(jnp.bfloat16)
    blended = jnp.einsum(
        "...hij,...jhe->...ihe", weights, values, preferred_element_type=jnp.float32
    )
    return blended.astype(jnp.bfloat16)


def relay_features(rows_now):
    return lax.all_to_all(rows_now, "seq", split_axis=0, concat_axis=0, tiled=True)


def pass_onward(rows_now):
    return passed_along(rows_now, "segment", 1)


def on_device(latents, w_qkv, w_out, mod_shift, mod_scale, mod_gate, counts):
    frames = lax.axis_size("seq")
    patches = latents.shape[2]
    narrow = latents.shape[3]
    span = patches // frames
    segment_rows = latents[0, 0]
    gathered = lax.all_gather(latents, "mp", axis=3, tiled=True)[0, 0]
    residual = relay_features(segment_rows.reshape(frames, span, narrow))
    widened = gathered.astype(jnp.float32)
    average = jnp.mean(widened, axis=-1, keepdims=True)
    centred = widened - average
    variance = jnp.mean(centred * centred, axis=-1, keepdims=True)
    modulated = (centred * lax.rsqrt(variance + EPS) * mod_scale[0] + mod_shift[0]).astype(
        jnp.bfloat16
    )
    columns = w_qkv.shape[2] * w_qkv.shape[3]
    depth = w_qkv.shape[1]
    spread = lax.all_to_all(
        modulated.reshape(patches, frames, depth).transpose(1, 0, 2),
        "seq", split_axis=0, concat_axis=0, tiled=True,
    ).reshape(frames * patches, depth)
    partial_in = jnp.dot(
        spread, w_qkv[0].reshape(depth, columns), preferred_element_type=jnp.float32
    ).astype(jnp.bfloat16)
    projected = lax.psum_scatter(partial_in, "seq", scatter_dimension=0, tiled=True)
    local_heads = w_qkv.shape[3] // HD
    projected = projected.reshape(patches, 3, local_heads, HD)
    frame_here = lax.axis_index("seq")
    clip_counts = counts[0]
    positions = jnp.arange(frames)

    def spatial(triple):
        count_here = jnp.sum(jnp.where(positions == frame_here, clip_counts, 0))
        usable = jnp.arange(patches) < count_here
        return masked_attention(triple[:, 0], triple[:, 1], triple[:, 2], usable)

    def temporal(triple):
        by_place = triple.reshape(frames, span, 3, local_heads, HD).transpose(1, 0, 2, 3, 4)
        location = frame_here * span + jnp.arange(span)
        usable = location[:, None] < clip_counts[None, :]
        blended = masked_attention(by_place[:, :, 0], by_place[:, :, 1], by_place[:, :, 2], usable)
        return blended.transpose(1, 0, 2, 3).reshape(patches, local_heads, HD)

    attended = lax.cond(lax.axis_index("segment") % 2 == 0, spatial, temporal, projected)
    attended = attended.reshape(patches, local_heads * HD)
    attended = lax.all_gather(attended, "seq", axis=0, tiled=True)
    member = lax.axis_index("mp")
    partials = jnp.dot(attended, w_out[0], preferred_element_type=jnp.float32).astype(jnp.bfloat16)
    width = w_out.shape[2]
    outgoing = partials.reshape(frames, frames, span, width).transpose(1, 0, 2, 3)
    arrived = lax.all_to_all(
        outgoing.reshape(frames, patches, width), "seq", split_axis=0, concat_axis=0, tiled=True
    )
    summed = lax.psum_scatter(arrived, "mp", scatter_dimension=0, tiled=True)
    summed = summed.transpose(1, 0, 2).reshape(patches, narrow).astype(jnp.float32)
    gate_here = lax.dynamic_slice_in_dim(mod_gate[0], member * narrow, narrow)
    updated = residual.reshape(patches, narrow).astype(jnp.float32) + gate_here * summed
    moved = pass_onward(updated.astype(jnp.bfloat16))
    return moved.reshape(1, 1, patches, narrow)


CHUNKS = 4


def whole_kernel(
    x, wq, wo, shift, scale, gate, counts, out,
    w_in, w_proj, tokens, mod, other, heads, sent, came, own, outs, parts, rest, halves, final,
    y_send, y_recv, wl, ws, wr, wol, x_send, x_recv, s_send, s_recv, f_send, f_recv,
    p_send, p_recv, ax_send, ax_recv, as_send, as_recv, af_send, af_recv,
    o_send, o_recv, r_send, r_recv, h_send, h_recv, z_send, z_recv,
):
    seg, j, m = lax.axis_index("segment"), lax.axis_index("seq"), lax.axis_index("mp")
    n_seg, n_seq, n_mp = lax.axis_size("segment"), lax.axis_size("seq"), lax.axis_size("mp")
    side, core = j // 2, j % 2
    sib = side * 2 + 1 - core
    across = (1 - side) * 2 + core
    after, before = lax.rem(seg + 1, n_seg), lax.rem(seg + n_seg - 1, n_seg)
    patches, narrow = x.shape
    span = patches // n_seq
    depth = wq.shape[1]
    wide = wq.shape[2] // 2
    step = wide // CHUNKS
    rows = 2 * patches

    def remote(src, dst, send, recv, seq=None, mp=None, segment=None):
        return pltpu.make_async_remote_copy(
            src_ref=src, dst_ref=dst, send_sem=send, recv_sem=recv,
            device_id=(seg if segment is None else segment, j if seq is None else seq,
                       m if mp is None else mp),
            device_id_type=pl.DeviceIdType.MESH,
        )

    def arrived(dst, recv, send):
        remote(dst, dst, send, recv, seq=sib).wait_recv()

    barrier = pltpu.get_barrier_semaphore()
    for dj in range(n_seq):
        for dm in range(n_mp):
            if dj or dm:
                pl.semaphore_signal(
                    barrier, inc=1,
                    device_id=(seg, lax.rem(j + dj, n_seq), lax.rem(m + dm, n_mp)),
                    device_id_type=pl.DeviceIdType.MESH,
                )

    pl.semaphore_signal(
        barrier, inc=1, device_id=(before, j, m), device_id_type=pl.DeviceIdType.MESH
    )

    def columns(which, g):
        return pl.ds(pl.multiple_of(which * wide + g * step, step), step)

    def w_local(g):
        return pltpu.make_async_copy(wq.at[:, :, columns(core, g)], w_in.at[g, :, core], wl.at[g])

    def w_remote(g):
        return remote(
            wq.at[:, :, columns(1 - core, g)], w_in.at[g, :, core], ws.at[g], wr.at[g], seq=sib
        )

    for g in range(CHUNKS):
        w_local(g).start()
    proj_copy = pltpu.make_async_copy(wo, w_proj, wol)
    proj_copy.start()

    pl.semaphore_wait(barrier, n_seq * n_mp)

    part = patches // CHUNKS

    def piece(i):
        return pl.ds(pl.multiple_of(i * part, part), part)

    def y_copy(i):
        return remote(x.at[piece(i)], other.at[piece(i)], y_send.at[i], y_recv.at[i], mp=1 - m)

    def rest_copy(d):
        b = lax.rem(j + d, n_seq)
        return remote(
            x.at[pl.ds(pl.multiple_of(b * span, span), span)],
            rest.at[pl.ds(pl.multiple_of(j * span, span), span)],
            r_send.at[d], r_recv.at[j], seq=b,
        )

    for i in range(CHUNKS):
        y_copy(i).start()
    for d in (2, 1, 3):
        rest_copy(d).start()
    here = pl.ds(pl.multiple_of(j * span, span), span)
    rest[here] = x[here]
    for g in range(CHUNKS):
        w_remote(g).start()

    def x_copy(i):
        return remote(
            mod.at[:, piece(i)], tokens.at[:, j, piece(i)], x_send.at[i], x_recv.at[i], seq=across
        )

    def s_copy(i):
        mine = tokens.at[:, j, piece(i)]
        return remote(mine, mine, s_send.at[i], s_recv.at[i], seq=sib)

    def f_copy(i):
        passed = tokens.at[:, across, piece(i)]
        return remote(passed, passed, f_send.at[i], f_recv.at[i], seq=sib)

    def norm_step(i, carry):
        y_copy(i).wait()
        a = x[piece(i)].astype(jnp.float32)
        b = other[piece(i)].astype(jnp.float32)
        mean = (jnp.sum(a, axis=-1, keepdims=True) + jnp.sum(b, axis=-1, keepdims=True)) / (
            2.0 * narrow
        )
        a, b = a - mean, b - mean
        variance = (
            jnp.sum(a * a, axis=-1, keepdims=True) + jnp.sum(b * b, axis=-1, keepdims=True)
        ) / (2.0 * narrow)
        rstd = lax.rsqrt(variance + EPS)
        keep = jnp.where(m == side, a, b) * rstd
        give = jnp.where(m == side, b, a) * rstd

        def modulate(values, which, q):
            at = pl.ds(pl.multiple_of(which * narrow + q * depth, depth), depth)
            block = values[:, q * depth:(q + 1) * depth]
            return (block * scale[:, at] + shift[:, at]).astype(jnp.bfloat16)

        for q in range(2):
            mod[q, piece(i)] = modulate(give, 1 - side, q)
        x_copy(i).start()
        for q in range(2):
            tokens[q, j, piece(i)] = modulate(keep, side, q)
        s_copy(i).start()
        return carry

    lax.fori_loop(0, CHUNKS, norm_step, 0)

    def project(which, g, i):
        total = jnp.zeros((rows, step), jnp.float32)
        for k in range(2):
            total = total + jnp.dot(
                tokens[k, pl.ds(which * 2, 2)].reshape(rows, depth), w_in[g, i, k],
                preferred_element_type=jnp.float32,
            )
        return total

    for i in range(CHUNKS):
        arrived(tokens.at[:, sib, piece(i)], s_recv.at[i], s_send.at[i])

    def own_step(g, carry):
        w_local(g).wait()
        w_remote(g).wait_send()
        arrived(w_in.at[g, :, 1 - core], wr.at[g], ws.at[g])
        for i in range(3):
            own[g, i] = project(side, g, i)
        arrived(tokens.at[:, across, piece(g)], x_recv.at[g], x_send.at[g])
        f_copy(g).start()
        return carry

    lax.fori_loop(0, CHUNKS, own_step, 0)

    far = (1 - side) * 2 + 1 - core
    for i in range(CHUNKS):
        arrived(tokens.at[:, far, piece(i)], f_recv.at[i], f_send.at[i])

    def p_copy(g):
        return remote(sent.at[g], came.at[g], p_send.at[g], p_recv.at[g], seq=across)

    def send_step(g, carry):
        for i in range(3):
            sent[g, i] = project(1 - side, g, i).astype(jnp.bfloat16)
        p_copy(g).start()
        return carry

    lax.fori_loop(0, CHUNKS, send_step, 0)

    spatial = 1 - lax.rem(seg, 2)

    def places(r, t):
        frame = jnp.zeros_like(r)
        for f in range(1, n_seq):
            frame = frame + jnp.where(r >= f * span, 1, 0)
        spot = r - frame * span
        frame = spatial * t + (1 - spatial) * frame
        patch = spatial * r + (1 - spatial) * (t * span + spot)
        limit = jnp.zeros_like(r)
        for f in range(n_seq):
            limit = jnp.where(frame == f, counts[0, f], limit)
        return patch < limit, (1 - spatial) * spot

    def ax_copy(g):
        here = heads.at[core, g, pl.ds(side * 2, 2)]
        return remote(here, here, ax_send.at[g], ax_recv.at[g], seq=across)

    def as_copy(g):
        here = heads.at[core, g, pl.ds(side * 2, 2)]
        return remote(here, here, as_send.at[g], as_recv.at[g], seq=sib)

    def af_copy(g):
        here = heads.at[core, g, pl.ds((1 - side) * 2, 2)]
        return remote(here, here, af_send.at[g], af_recv.at[g], seq=sib)

    def forward(g):
        arrived(heads.at[core, g, pl.ds((1 - side) * 2, 2)], ax_recv.at[g], af_send.at[g])
        af_copy(g).start()

    factor = 1.0 / math.sqrt(HD)

    def attend_step(g, carry):
        p_copy(g).wait_send()
        arrived(came.at[g], p_recv.at[g], p_send.at[g])
        for b in range(2):
            t = side * 2 + b
            valid_q, spot_q = places(lax.broadcasted_iota(jnp.int32, (patches, 1), 0), t)
            valid_k, spot_k = places(lax.broadcasted_iota(jnp.int32, (1, patches), 1), t)
            allowed = jnp.logical_and(jnp.logical_and(valid_q, valid_k), spot_q == spot_k)
            spare = jnp.where(valid_q, 0.0, 1.0)
            mine = pl.ds(b * patches, patches)
            q, k, v = [
                (own[g, i, mine] + came[g, i, mine].astype(jnp.float32)).astype(jnp.bfloat16)
                for i in range(3)
            ]
            for h in range(step // HD):
                at = slice(h * HD, (h + 1) * HD)
                scores = lax.dot_general(
                    q[:, at], k[:, at], (((1,), (1,)), ((), ())),
                    preferred_element_type=jnp.float32,
                ) * factor
                masked = jnp.where(allowed, scores, NEG_FILL)
                highest = jnp.max(masked, axis=-1, keepdims=True)
                raised = jnp.where(allowed, jnp.exp(masked - highest), 0.0)
                total = jnp.sum(raised, axis=-1, keepdims=True) + spare
                weights = (raised / total).astype(jnp.bfloat16)
                blended = jnp.dot(weights, v[:, at], preferred_element_type=jnp.float32)
                heads[core, g, t, :, :, at] = blended.astype(jnp.bfloat16).reshape(n_seq, span, HD)
        ax_copy(g).start()
        as_copy(g).start()

        @pl.when(g > 0)
        def _():
            forward(g - 1)

        return carry

    lax.fori_loop(0, CHUNKS, attend_step, 0)
    forward(CHUNKS - 1)
    for g in range(CHUNKS):
        arrived(heads.at[1 - core, g, pl.ds(side * 2, 2)], as_recv.at[g], as_send.at[g])
        arrived(heads.at[1 - core, g, pl.ds((1 - side) * 2, 2)], af_recv.at[g], af_send.at[g])
    proj_copy.wait()

    gate_here = gate[:, pl.ds(pl.multiple_of(j * depth, depth), depth)]

    rounds = n_seq // 2
    part_rows = patches // 2

    def strip(r):
        return pl.ds(r * part_rows, part_rows)

    def o_copy(b, slot, r):
        return remote(
            outs.at[slot, strip(r)], parts.at[j, strip(r)],
            o_send.at[slot, r], o_recv.at[j, r], seq=b,
        )

    def out_part(pair, r):
        left = jnp.concatenate(
            [
                heads[k, g, 2 * r:2 * r + 2, pl.ds(pair * 2, 2)].reshape(2 * part_rows, step)
                for k in range(2) for g in range(CHUNKS)
            ],
            axis=-1,
        )
        branch = jnp.dot(left, w_proj[...], preferred_element_type=jnp.float32)
        return (branch * gate_here).astype(jnp.bfloat16).reshape(2, 2, span, depth)

    for r in range(rounds):
        result = out_part(1 - side, r)
        for k in range(2):
            outs[k, strip(r)] = result[:, k].reshape(part_rows, depth)
            o_copy((1 - side) * 2 + k, k, r).start()
    for r in range(rounds):
        result = out_part(side, r)
        for k in range(2):
            @pl.when(core == k)
            def _():
                parts[j, strip(r)] = result[:, k].reshape(part_rows, depth)

            @pl.when(core != k)
            def _():
                outs[2, strip(r)] = result[:, k].reshape(part_rows, depth)
        o_copy(sib, 2, r).start()

    for d in range(1, n_seq):
        f = lax.rem(j + d, n_seq)
        arrived(
            rest.at[pl.ds(pl.multiple_of(f * span, span), span)], r_recv.at[f], r_send.at[d]
        )

    def h_copy(q, r):
        return remote(
            parts.at[(1 - m) * 2 + q, strip(r)], halves.at[q, strip(r)],
            h_send.at[q, r], h_recv.at[q, r], mp=1 - m,
        )

    def z_copy(q, r):
        at = pl.ds(q * depth, depth)
        return remote(
            final.at[strip(r), at], out.at[strip(r), at],
            z_send.at[q, r], z_recv.at[q, r], segment=after,
        )

    def got_part(f, r):
        @pl.when(f != j)
        def _():
            arrived(parts.at[f, strip(r)], o_recv.at[f, r], o_send.at[0, r])

    for r in range(rounds):
        for q in range(2):
            got_part((1 - m) * 2 + q, r)
            h_copy(q, r).start()
        for q in range(2):
            got_part(m * 2 + q, r)
            h_copy(q, r).wait_recv()
            at = slice(q * depth, (q + 1) * depth)
            final[strip(r), at] = (
                rest[strip(r), at].astype(jnp.float32)
                + parts[m * 2 + q, strip(r)].astype(jnp.float32)
                + halves[q, strip(r)].astype(jnp.float32)
            ).astype(jnp.bfloat16)
            z_copy(q, r).start()
    for r in range(rounds):
        for q in range(2):
            h_copy(q, r).wait_send()
            z_copy(q, r).wait()
        for slot in range(3):
            o_copy(sib, slot, r).wait_send()
    for d in range(1, n_seq):
        rest_copy(d).wait_send()
    for g in range(CHUNKS):
        x_copy(g).wait_send()
        s_copy(g).wait_send()
        f_copy(g).wait_send()
        ax_copy(g).wait_send()
        as_copy(g).wait_send()
        af_copy(g).wait_send()


def in_one_kernel(latents, w_qkv, w_out, mod_shift, mod_scale, mod_gate, counts):
    patches, narrow = latents.shape[2:]
    n_seq = lax.axis_size("seq")
    depth, heads_wide = w_qkv.shape[1], w_qkv.shape[3]
    wide = heads_wide // 2
    step = wide // CHUNKS
    span = patches // n_seq
    rows = 2 * patches
    vmem = pl.BlockSpec(memory_space=pltpu.VMEM)
    dma = pltpu.SemaphoreType.DMA
    bf16 = jnp.bfloat16
    moved = pl.pallas_call(
        whole_kernel,
        out_shape=jax.ShapeDtypeStruct((patches, narrow), bf16),
        in_specs=[
            vmem, pl.BlockSpec(memory_space=pl.ANY), pl.BlockSpec(memory_space=pl.ANY),
            vmem, vmem, vmem, pl.BlockSpec(memory_space=pltpu.SMEM),
        ],
        out_specs=vmem,
        scratch_shapes=[
            pltpu.VMEM((CHUNKS, 3, 2, depth, step), bf16),
            pltpu.VMEM(w_out.shape[1:], bf16),
            pltpu.VMEM((2, n_seq, patches, depth), bf16),
            pltpu.VMEM((2, patches, depth), bf16),
            pltpu.VMEM((patches, narrow), bf16),
            pltpu.VMEM((2, CHUNKS, n_seq, n_seq, span, step), bf16),
            pltpu.VMEM((CHUNKS, 3, rows, step), bf16),
            pltpu.VMEM((CHUNKS, 3, rows, step), bf16),
            pltpu.VMEM((CHUNKS, 3, rows, step), jnp.float32),
            pltpu.VMEM((3, patches, depth), bf16),
            pltpu.VMEM((n_seq, patches, depth), bf16),
            pltpu.VMEM((patches, narrow), bf16),
            pltpu.VMEM((2, patches, depth), bf16),
            pltpu.VMEM((patches, narrow), bf16),
            dma((CHUNKS,)), dma((CHUNKS,)), dma((CHUNKS,)), dma((CHUNKS,)), dma((CHUNKS,)), dma,
            dma((CHUNKS,)), dma((CHUNKS,)), dma((CHUNKS,)), dma((CHUNKS,)),
            dma((CHUNKS,)), dma((CHUNKS,)),
            dma((CHUNKS,)), dma((CHUNKS,)), dma((CHUNKS,)), dma((CHUNKS,)),
            dma((CHUNKS,)), dma((CHUNKS,)), dma((CHUNKS,)), dma((CHUNKS,)),
            dma((3, 2)), dma((n_seq, 2)), dma((n_seq,)), dma((n_seq,)),
            dma((2, 2)), dma((2, 2)), dma((2, 2)), dma((2, 2)),
        ],
        compiler_params=pltpu.CompilerParams(
            collective_id=0, has_side_effects=True, vmem_limit_bytes=60 * 2**20
        ),
    )(
        latents[0, 0], w_qkv[0].transpose(1, 0, 2), w_out[0],
        mod_shift, mod_scale, mod_gate, counts,
    )
    return moved.reshape(latents.shape)


def solution(mesh):
    square = mesh.shape["seq"] == 4 and mesh.shape["mp"] == 2
    return jax.shard_map(
        in_one_kernel if square else on_device,
        mesh=mesh,
        in_specs=(
            P("segment", "seq", None, "mp"),
            P("segment", "seq", None, "mp"),
            P("segment", "mp", "seq"),
            P("segment", None),
            P("segment", None),
            P("segment", None),
            P("segment", None),
        ),
        out_specs=P("segment", "seq", None, "mp"),
        check_vma=False,
    )
```

```python
import math

import jax
import jax.numpy as jnp
from jax import lax
from jax.experimental import pallas as pl
from jax.experimental.pallas import tpu as pltpu
from jax.sharding import PartitionSpec as P

HD = 128


EPS = 1e-06
NEG_FILL = -1e30


def passed_along(x, axis, by):
    length = lax.axis_size(axis)
    return lax.ppermute(x, axis, [(i, (i + by) % length) for i in range(length)])


def masked_attention(queries, keys_in, values, usable):
    factor = 1.0 / math.sqrt(queries.shape[-1])
    scores = (
        jnp.einsum("...ihe,...jhe->...hij", queries, keys_in, preferred_element_type=jnp.float32)
        * factor
    )
    allowed = usable[..., None, :, None] & usable[..., None, None, :]
    masked = jnp.where(allowed, scores, NEG_FILL)
    highest = jnp.max(masked, axis=-1, keepdims=True)
    raised = jnp.where(allowed, jnp.exp(masked - highest), 0.0)
    spare_one = jnp.where(usable, 0.0, 1.0)[..., None, :, None]
    weights = (raised / (jnp.sum(raised, axis=-1, keepdims=True) + spare_one)).astype(jnp.bfloat16)
    blended = jnp.einsum(
        "...hij,...jhe->...ihe", weights, values, preferred_element_type=jnp.float32
    )
    return blended.astype(jnp.bfloat16)


def relay_features(rows_now):
    return lax.all_to_all(rows_now, "seq", split_axis=0, concat_axis=0, tiled=True)


def pass_onward(rows_now):
    return passed_along(rows_now, "segment", 1)


def on_device(latents, w_qkv, w_out, mod_shift, mod_scale, mod_gate, counts):
    frames = lax.axis_size("seq")
    patches = latents.shape[2]
    narrow = latents.shape[3]
    span = patches // frames
    segment_rows = latents[0, 0]
    gathered = lax.all_gather(latents, "mp", axis=3, tiled=True)[0, 0]
    residual = relay_features(segment_rows.reshape(frames, span, narrow))
    widened = gathered.astype(jnp.float32)
    average = jnp.mean(widened, axis=-1, keepdims=True)
    centred = widened - average
    variance = jnp.mean(centred * centred, axis=-1, keepdims=True)
    modulated = (centred * lax.rsqrt(variance + EPS) * mod_scale[0] + mod_shift[0]).astype(
        jnp.bfloat16
    )
    columns = w_qkv.shape[2] * w_qkv.shape[3]
    depth = w_qkv.shape[1]
    spread = lax.all_to_all(
        modulated.reshape(patches, frames, depth).transpose(1, 0, 2),
        "seq", split_axis=0, concat_axis=0, tiled=True,
    ).reshape(frames * patches, depth)
    partial_in = jnp.dot(
        spread, w_qkv[0].reshape(depth, columns), preferred_element_type=jnp.float32
    ).astype(jnp.bfloat16)
    projected = lax.psum_scatter(partial_in, "seq", scatter_dimension=0, tiled=True)
    local_heads = w_qkv.shape[3] // HD
    projected = projected.reshape(patches, 3, local_heads, HD)
    frame_here = lax.axis_index("seq")
    clip_counts = counts[0]
    positions = jnp.arange(frames)

    def spatial(triple):
        count_here = jnp.sum(jnp.where(positions == frame_here, clip_counts, 0))
        usable = jnp.arange(patches) < count_here
        return masked_attention(triple[:, 0], triple[:, 1], triple[:, 2], usable)

    def temporal(triple):
        by_place = triple.reshape(frames, span, 3, local_heads, HD).transpose(1, 0, 2, 3, 4)
        location = frame_here * span + jnp.arange(span)
        usable = location[:, None] < clip_counts[None, :]
        blended = masked_attention(by_place[:, :, 0], by_place[:, :, 1], by_place[:, :, 2], usable)
        return blended.transpose(1, 0, 2, 3).reshape(patches, local_heads, HD)

    attended = lax.cond(lax.axis_index("segment") % 2 == 0, spatial, temporal, projected)
    attended = attended.reshape(patches, local_heads * HD)
    attended = lax.all_gather(attended, "seq", axis=0, tiled=True)
    member = lax.axis_index("mp")
    partials = jnp.dot(attended, w_out[0], preferred_element_type=jnp.float32).astype(jnp.bfloat16)
    width = w_out.shape[2]
    outgoing = partials.reshape(frames, frames, span, width).transpose(1, 0, 2, 3)
    arrived = lax.all_to_all(
        outgoing.reshape(frames, patches, width), "seq", split_axis=0, concat_axis=0, tiled=True
    )
    summed = lax.psum_scatter(arrived, "mp", scatter_dimension=0, tiled=True)
    summed = summed.transpose(1, 0, 2).reshape(patches, narrow).astype(jnp.float32)
    gate_here = lax.dynamic_slice_in_dim(mod_gate[0], member * narrow, narrow)
    updated = residual.reshape(patches, narrow).astype(jnp.float32) + gate_here * summed
    moved = pass_onward(updated.astype(jnp.bfloat16))
    return moved.reshape(1, 1, patches, narrow)


CHUNKS = 4


def whole_kernel(
    x, wq, wo, shift, scale, gate, counts, out,
    w_in, w_proj, tokens, mod, other, heads, sent, came, own, outs, parts, rest, halves, final,
    y_send, y_recv, wl, ws, wr, wol, x_send, x_recv, s_send, s_recv, f_send, f_recv,
    p_send, p_recv, ax_send, ax_recv, as_send, as_recv, af_send, af_recv,
    o_send, o_recv, r_send, r_recv, h_send, h_recv, z_send, z_recv,
):
    seg, j, m = lax.axis_index("segment"), lax.axis_index("seq"), lax.axis_index("mp")
    n_seg, n_seq, n_mp = lax.axis_size("segment"), lax.axis_size("seq"), lax.axis_size("mp")
    side, core = j // 2, j % 2
    sib = side * 2 + 1 - core
    across = (1 - side) * 2 + core
    after, before = lax.rem(seg + 1, n_seg), lax.rem(seg + n_seg - 1, n_seg)
    patches, narrow = x.shape
    span = patches // n_seq
    depth = wq.shape[1]
    wide = wq.shape[2] // 2
    step = wide // CHUNKS
    rows = 2 * patches

    def remote(src, dst, send, recv, seq=None, mp=None, segment=None):
        return pltpu.make_async_remote_copy(
            src_ref=src, dst_ref=dst, send_sem=send, recv_sem=recv,
            device_id=(seg if segment is None else segment, j if seq is None else seq,
                       m if mp is None else mp),
            device_id_type=pl.DeviceIdType.MESH,
        )

    def arrived(dst, recv, send):
        remote(dst, dst, send, recv, seq=sib).wait_recv()

    barrier = pltpu.get_barrier_semaphore()
    for dj in range(n_seq):
        for dm in range(n_mp):
            if dj or dm:
                pl.semaphore_signal(
                    barrier, inc=1,
                    device_id=(seg, lax.rem(j + dj, n_seq), lax.rem(m + dm, n_mp)),
                    device_id_type=pl.DeviceIdType.MESH,
                )

    pl.semaphore_signal(
        barrier, inc=1, device_id=(before, j, m), device_id_type=pl.DeviceIdType.MESH
    )

    def columns(which, g):
        return pl.ds(pl.multiple_of(which * wide + g * step, step), step)

    def w_local(g):
        return pltpu.make_async_copy(wq.at[:, :, columns(core, g)], w_in.at[g, :, core], wl.at[g])

    def w_remote(g):
        return remote(
            wq.at[:, :, columns(1 - core, g)], w_in.at[g, :, core], ws.at[g], wr.at[g], seq=sib
        )

    for g in range(CHUNKS):
        w_local(g).start()
    proj_copy = pltpu.make_async_copy(wo, w_proj, wol)
    proj_copy.start()

    pl.semaphore_wait(barrier, n_seq * n_mp)

    part = patches // CHUNKS

    def piece(i):
        return pl.ds(pl.multiple_of(i * part, part), part)

    def y_copy(i):
        return remote(x.at[piece(i)], other.at[piece(i)], y_send.at[i], y_recv.at[i], mp=1 - m)

    def rest_copy(d):
        b = lax.rem(j + d, n_seq)
        return remote(
            x.at[pl.ds(pl.multiple_of(b * span, span), span)],
            rest.at[pl.ds(pl.multiple_of(j * span, span), span)],
            r_send.at[d], r_recv.at[j], seq=b,
        )

    for i in range(CHUNKS):
        y_copy(i).start()
    for d in (2, 1, 3):
        rest_copy(d).start()
    here = pl.ds(pl.multiple_of(j * span, span), span)
    rest[here] = x[here]
    for g in range(CHUNKS):
        w_remote(g).start()

    def x_copy(i):
        return remote(
            mod.at[:, piece(i)], tokens.at[:, j, piece(i)], x_send.at[i], x_recv.at[i], seq=across
        )

    def s_copy(i):
        mine = tokens.at[:, j, piece(i)]
        return remote(mine, mine, s_send.at[i], s_recv.at[i], seq=sib)

    def f_copy(i):
        passed = tokens.at[:, across, piece(i)]
        return remote(passed, passed, f_send.at[i], f_recv.at[i], seq=sib)

    def norm_step(i, carry):
        y_copy(i).wait()
        a = x[piece(i)].astype(jnp.float32)
        b = other[piece(i)].astype(jnp.float32)
        mean = (jnp.sum(a, axis=-1, keepdims=True) + jnp.sum(b, axis=-1, keepdims=True)) / (
            2.0 * narrow
        )
        a, b = a - mean, b - mean
        variance = (
            jnp.sum(a * a, axis=-1, keepdims=True) + jnp.sum(b * b, axis=-1, keepdims=True)
        ) / (2.0 * narrow)
        rstd = lax.rsqrt(variance + EPS)
        keep = jnp.where(m == side, a, b) * rstd
        give = jnp.where(m == side, b, a) * rstd

        def modulate(values, which, q):
            at = pl.ds(pl.multiple_of(which * narrow + q * depth, depth), depth)
            block = values[:, q * depth:(q + 1) * depth]
            return (block * scale[:, at] + shift[:, at]).astype(jnp.bfloat16)

        for q in range(2):
            mod[q, piece(i)] = modulate(give, 1 - side, q)
        x_copy(i).start()
        for q in range(2):
            tokens[q, j, piece(i)] = modulate(keep, side, q)
        s_copy(i).start()
        return carry

    lax.fori_loop(0, CHUNKS, norm_step, 0)

    def project(which, g, i):
        total = jnp.zeros((rows, step), jnp.float32)
        for k in range(2):
            total = total + jnp.dot(
                tokens[k, pl.ds(which * 2, 2)].reshape(rows, depth), w_in[g, i, k],
                preferred_element_type=jnp.float32,
            )
        return total

    for i in range(CHUNKS):
        arrived(tokens.at[:, sib, piece(i)], s_recv.at[i], s_send.at[i])

    def own_step(g, carry):
        w_local(g).wait()
        w_remote(g).wait_send()
        arrived(w_in.at[g, :, 1 - core], wr.at[g], ws.at[g])
        for i in range(3):
            own[g, i] = project(side, g, i)
        arrived(tokens.at[:, across, piece(g)], x_recv.at[g], x_send.at[g])
        f_copy(g).start()
        return carry

    lax.fori_loop(0, CHUNKS, own_step, 0)

    far = (1 - side) * 2 + 1 - core
    for i in range(CHUNKS):
        arrived(tokens.at[:, far, piece(i)], f_recv.at[i], f_send.at[i])

    def p_copy(g):
        return remote(sent.at[g], came.at[g], p_send.at[g], p_recv.at[g], seq=across)

    def send_step(g, carry):
        for i in range(3):
            sent[g, i] = project(1 - side, g, i).astype(jnp.bfloat16)
        p_copy(g).start()
        return carry

    lax.fori_loop(0, CHUNKS, send_step, 0)

    spatial = 1 - lax.rem(seg, 2)

    def places(r, t):
        frame = jnp.zeros_like(r)
        for f in range(1, n_seq):
            frame = frame + jnp.where(r >= f * span, 1, 0)
        spot = r - frame * span
        frame = spatial * t + (1 - spatial) * frame
        patch = spatial * r + (1 - spatial) * (t * span + spot)
        limit = jnp.zeros_like(r)
        for f in range(n_seq):
            limit = jnp.where(frame == f, counts[0, f], limit)
        return patch < limit, (1 - spatial) * spot

    def ax_copy(g):
        here = heads.at[core, g, pl.ds(side * 2, 2)]
        return remote(here, here, ax_send.at[g], ax_recv.at[g], seq=across)

    def as_copy(g):
        here = heads.at[core, g, pl.ds(side * 2, 2)]
        return remote(here, here, as_send.at[g], as_recv.at[g], seq=sib)

    def af_copy(g):
        here = heads.at[core, g, pl.ds((1 - side) * 2, 2)]
        return remote(here, here, af_send.at[g], af_recv.at[g], seq=sib)

    def forward(g):
        arrived(heads.at[core, g, pl.ds((1 - side) * 2, 2)], ax_recv.at[g], af_send.at[g])
        af_copy(g).start()

    factor = 1.0 / math.sqrt(HD)

    def attend_step(g, carry):
        p_copy(g).wait_send()
        arrived(came.at[g], p_recv.at[g], p_send.at[g])
        for b in range(2):
            t = side * 2 + b
            valid_q, spot_q = places(lax.broadcasted_iota(jnp.int32, (patches, 1), 0), t)
            valid_k, spot_k = places(lax.broadcasted_iota(jnp.int32, (1, patches), 1), t)
            allowed = jnp.logical_and(jnp.logical_and(valid_q, valid_k), spot_q == spot_k)
            spare = jnp.where(valid_q, 0.0, 1.0)
            mine = pl.ds(b * patches, patches)
            q, k, v = [
                (own[g, i, mine] + came[g, i, mine].astype(jnp.float32)).astype(jnp.bfloat16)
                for i in range(3)
            ]
            for h in range(step // HD):
                at = slice(h * HD, (h + 1) * HD)
                scores = lax.dot_general(
                    q[:, at], k[:, at], (((1,), (1,)), ((), ())),
                    preferred_element_type=jnp.float32,
                ) * factor
                masked = jnp.where(allowed, scores, NEG_FILL)
                highest = jnp.max(masked, axis=-1, keepdims=True)
                raised = jnp.where(allowed, jnp.exp(masked - highest), 0.0)
                total = jnp.sum(raised, axis=-1, keepdims=True) + spare
                weights = (raised / total).astype(jnp.bfloat16)
                blended = jnp.dot(weights, v[:, at], preferred_element_type=jnp.float32)
                heads[core, g, t, :, :, at] = blended.astype(jnp.bfloat16).reshape(n_seq, span, HD)
        ax_copy(g).start()
        as_copy(g).start()

        @pl.when(g > 0)
        def _():
            forward(g - 1)

        return carry

    lax.fori_loop(0, CHUNKS, attend_step, 0)
    forward(CHUNKS - 1)
    for g in range(CHUNKS):
        arrived(heads.at[1 - core, g, pl.ds(side * 2, 2)], as_recv.at[g], as_send.at[g])
        arrived(heads.at[1 - core, g, pl.ds((1 - side) * 2, 2)], af_recv.at[g], af_send.at[g])
    proj_copy.wait()

    gate_here = gate[:, pl.ds(pl.multiple_of(j * depth, depth), depth)]

    rounds = n_seq
    part_rows = span

    def strip(r):
        return pl.ds(r * part_rows, part_rows)

    def o_copy(b, slot, r):
        return remote(
            outs.at[slot, strip(r)], parts.at[j, strip(r)],
            o_send.at[slot, r], o_recv.at[j, r], seq=b,
        )

    def out_part(pair, r):
        left = jnp.concatenate(
            [
                heads[k, g, r, pl.ds(pair * 2, 2)].reshape(2 * part_rows, step)
                for k in range(2) for g in range(CHUNKS)
            ],
            axis=-1,
        )
        branch = jnp.dot(left, w_proj[...], preferred_element_type=jnp.float32)
        return (branch * gate_here).astype(jnp.bfloat16).reshape(2, span, depth)

    for r in range(rounds):
        result = out_part(1 - side, r)
        for k in range(2):
            outs[k, strip(r)] = result[k]
            o_copy((1 - side) * 2 + k, k, r).start()

    for d in range(1, n_seq):
        f = lax.rem(j + d, n_seq)
        arrived(
            rest.at[pl.ds(pl.multiple_of(f * span, span), span)], r_recv.at[f], r_send.at[d]
        )

    def h_copy(q, r):
        return remote(
            parts.at[(1 - m) * 2 + q, strip(r)], halves.at[q, strip(r)],
            h_send.at[q, r], h_recv.at[q, r], mp=1 - m,
        )

    def z_copy(q, r):
        at = pl.ds(q * depth, depth)
        return remote(
            final.at[strip(r), at], out.at[strip(r), at],
            z_send.at[q, r], z_recv.at[q, r], segment=after,
        )

    def got_part(f, r):
        @pl.when(f != j)
        def _():
            arrived(parts.at[f, strip(r)], o_recv.at[f, r], o_send.at[0, r])

    def finish(r):
        for q in range(2):
            got_part(m * 2 + q, r)
            h_copy(q, r).wait_recv()
            at = slice(q * depth, (q + 1) * depth)
            final[strip(r), at] = (
                rest[strip(r), at].astype(jnp.float32)
                + parts[m * 2 + q, strip(r)].astype(jnp.float32)
                + halves[q, strip(r)].astype(jnp.float32)
            ).astype(jnp.bfloat16)
            z_copy(q, r).start()

    for r in range(rounds):
        result = out_part(side, r)
        for k in range(2):
            @pl.when(core == k)
            def _():
                parts[j, strip(r)] = result[k]

            @pl.when(core != k)
            def _():
                outs[2, strip(r)] = result[k]
        o_copy(sib, 2, r).start()
        for q in range(2):
            got_part((1 - m) * 2 + q, r)
            h_copy(q, r).start()
        if r:
            finish(r - 1)
    finish(rounds - 1)
    for r in range(rounds):
        for q in range(2):
            h_copy(q, r).wait_send()
            z_copy(q, r).wait()
        for slot in range(3):
            o_copy(sib, slot, r).wait_send()
    for d in range(1, n_seq):
        rest_copy(d).wait_send()
    for g in range(CHUNKS):
        x_copy(g).wait_send()
        s_copy(g).wait_send()
        f_copy(g).wait_send()
        ax_copy(g).wait_send()
        as_copy(g).wait_send()
        af_copy(g).wait_send()


def in_one_kernel(latents, w_qkv, w_out, mod_shift, mod_scale, mod_gate, counts):
    patches, narrow = latents.shape[2:]
    n_seq = lax.axis_size("seq")
    depth, heads_wide = w_qkv.shape[1], w_qkv.shape[3]
    wide = heads_wide // 2
    step = wide // CHUNKS
    span = patches // n_seq
    rows = 2 * patches
    vmem = pl.BlockSpec(memory_space=pltpu.VMEM)
    dma = pltpu.SemaphoreType.DMA
    bf16 = jnp.bfloat16
    moved = pl.pallas_call(
        whole_kernel,
        out_shape=jax.ShapeDtypeStruct((patches, narrow), bf16),
        in_specs=[
            vmem, pl.BlockSpec(memory_space=pl.ANY), pl.BlockSpec(memory_space=pl.ANY),
            vmem, vmem, vmem, pl.BlockSpec(memory_space=pltpu.SMEM),
        ],
        out_specs=vmem,
        scratch_shapes=[
            pltpu.VMEM((CHUNKS, 3, 2, depth, step), bf16),
            pltpu.VMEM(w_out.shape[1:], bf16),
            pltpu.VMEM((2, n_seq, patches, depth), bf16),
            pltpu.VMEM((2, patches, depth), bf16),
            pltpu.VMEM((patches, narrow), bf16),
            pltpu.VMEM((2, CHUNKS, n_seq, n_seq, span, step), bf16),
            pltpu.VMEM((CHUNKS, 3, rows, step), bf16),
            pltpu.VMEM((CHUNKS, 3, rows, step), bf16),
            pltpu.VMEM((CHUNKS, 3, rows, step), jnp.float32),
            pltpu.VMEM((3, patches, depth), bf16),
            pltpu.VMEM((n_seq, patches, depth), bf16),
            pltpu.VMEM((patches, narrow), bf16),
            pltpu.VMEM((2, patches, depth), bf16),
            pltpu.VMEM((patches, narrow), bf16),
            dma((CHUNKS,)), dma((CHUNKS,)), dma((CHUNKS,)), dma((CHUNKS,)), dma((CHUNKS,)), dma,
            dma((CHUNKS,)), dma((CHUNKS,)), dma((CHUNKS,)), dma((CHUNKS,)),
            dma((CHUNKS,)), dma((CHUNKS,)),
            dma((CHUNKS,)), dma((CHUNKS,)), dma((CHUNKS,)), dma((CHUNKS,)),
            dma((CHUNKS,)), dma((CHUNKS,)), dma((CHUNKS,)), dma((CHUNKS,)),
            dma((3, n_seq)), dma((n_seq, n_seq)), dma((n_seq,)), dma((n_seq,)),
            dma((2, n_seq)), dma((2, n_seq)), dma((2, n_seq)), dma((2, n_seq)),
        ],
        compiler_params=pltpu.CompilerParams(
            collective_id=0, has_side_effects=True, vmem_limit_bytes=60 * 2**20
        ),
    )(
        latents[0, 0], w_qkv[0].transpose(1, 0, 2), w_out[0],
        mod_shift, mod_scale, mod_gate, counts,
    )
    return moved.reshape(latents.shape)


def solution(mesh):
    square = mesh.shape["seq"] == 4 and mesh.shape["mp"] == 2
    return jax.shard_map(
        in_one_kernel if square else on_device,
        mesh=mesh,
        in_specs=(
            P("segment", "seq", None, "mp"),
            P("segment", "seq", None, "mp"),
            P("segment", "mp", "seq"),
            P("segment", None),
            P("segment", None),
            P("segment", None),
            P("segment", None),
        ),
        out_specs=P("segment", "seq", None, "mp"),
        check_vma=False,
    )
```
